32 devices in a mesh: row: 8 (over y, x, core), col: 4 (over z).
Axes of the slice: x: 2, y: 2, z: 4, core: 2. Of those that a mesh axis runs over, the one named last changes fastest.
Arguments:
- u_factors: bfloat16 [24, 24, 1024, 128], P('row', 'col'), may hold values from -0.109375 to 0.109375
- v_factors: bfloat16 [24, 24, 1024, 128], P('row', 'col'), may hold values from -0.1875 to 0.1875
- tile_scales: float32 [24, 24, 128], P('row', 'col'), may hold values from 0.3 to 3
- rank_class: int32 [24, 24], P('row', 'col'), may hold values from 0 to 3, as said below
- slopes: float32 [64, 24576], P(None, 'row'), may hold values from -40 to 40
Outputs:
- solution_field: float32 [64, 24576], P(None, 'col')
- residual: float32 [64, 24576], P(None, 'col')
The draws below stay inside these ranges and needn't reach their ends.
Inputs may be any that keep to these rules, and one draw needn't show every extreme that they name: `rank_class`: class k gives a tile of rank 128 / 8 * 2**k; tiles of one device tend to share high or low classes.
All inputs are finite; a program needn't handle non-finite values.
Results may differ from the reference program's by a relative error of at most 0.017.
Values may be sent and summed in bfloat16 or wider, within the bound.
A program may use at most 64 MiB of HBM per device.

```python
import math
import jax
import jax.numpy as jnp
from jax import lax

TILE = 1024
RMAX = 128
TR_DEV = 3
TC_DEV = 6
FRAMES = 64
ITERS = 2
TILE_ROWS = 24
TILE_COLS = 24
SLOPES = 24576
MODES = 24576


def draw_rank_class(key, part):
    key_rows, key_cols, key_noise = jax.random.split(key, 3)
    row_level = jax.random.randint(key_rows, (TILE_ROWS // TR_DEV,), 0, 3)
    col_level = jax.random.randint(key_cols, (TILE_COLS // TC_DEV,), 0, 2)
    noise = jax.random.randint(key_noise, (TILE_ROWS, TILE_COLS), -2, 2)
    row_blocks = jnp.arange(TILE_ROWS) // TR_DEV
    col_blocks = jnp.arange(TILE_COLS) // TC_DEV
    levels = row_level[row_blocks][:, None] + col_level[col_blocks][None, :] + noise
    classes = jnp.clip(levels, 0, 3)
    classes = classes.at[0, 0].set(3)
    classes = classes.at[TILE_ROWS - 1, TILE_COLS - 1].set(0)
    return classes.astype(jnp.int32)


def draw_slopes(key, part):
    key_frames, key_slopes, key_entries = jax.random.split(key, 3)
    frame_scale = jnp.exp(jax.random.uniform(key_frames, (FRAMES, 1), jnp.float32, math.log(0.3), math.log(3.0)))
    slope_scale = jnp.exp(jax.random.uniform(key_slopes, (1, SLOPES), jnp.float32, math.log(0.3), math.log(3.0)))
    values = jnp.clip(jax.random.normal(key_entries, (FRAMES, SLOPES), jnp.float32), -4.0, 4.0)
    return (values * frame_scale * slope_scale).astype(jnp.float32)


def block_scale(rng, extent, cuts, least, largest):
    def one(position, parts):
        steps = jax.random.uniform(jax.random.fold_in(jax.random.fold_in(rng, 6), position), (parts,), jnp.float32, least / len(cuts), largest / len(cuts))
        return jnp.repeat(jnp.exp(steps), extent[position] // parts).reshape((-1,) + (1,) * (len(extent) - position - 1))

    factor_of = one(*cuts[0])
    for cut in cuts[1:]:
        factor_of = factor_of * one(*cut)
    return factor_of


def centred(own_key, shape, deviation, most, cuts=(), dtype=jnp.bfloat16):
    loudness = block_scale(own_key, shape, cuts, -0.22, 0.18) if cuts else 1.0
    drawn = jax.random.normal(own_key, shape, jnp.float32) * deviation * loudness
    return jnp.minimum(jnp.maximum(drawn, -most), most).astype(dtype)


def setup_inputs(seed: int = 0) -> dict:
    streams_of = jax.random.split(jax.random.key(seed), 6)
    return {
        "u_factors": centred(streams_of[0], (TILE_ROWS, TILE_COLS, TILE, RMAX), (RMAX * TILE_ROWS) ** -0.5, 0.109375, ((0, 8), (1, 4))),
        "v_factors": centred(streams_of[1], (TILE_ROWS, TILE_COLS, TILE, RMAX), TILE ** -0.5, 0.1875, ((0, 8), (1, 4))),
        "tile_scales": jnp.clip(jnp.exp(math.log(3.0) - 2.3025851 * jax.random.uniform(streams_of[2], (TILE_ROWS, TILE_COLS, RMAX), jnp.float32) ** block_scale(streams_of[2], (TILE_ROWS, TILE_COLS, RMAX), ((0, 8), (1, 4)), -0.2, 0.2)), 0.3, 3.0),
        "rank_class": draw_rank_class(jax.random.fold_in(streams_of[5], 71), 0),
        "slopes": draw_slopes(jax.random.fold_in(streams_of[5], 71), 0),
    }


damping = 0.1
epsilon = 1e-6


def rank_weights(tile_scales, rank_class):
    max_rank = tile_scales.shape[-1]
    ranks = jnp.left_shift(jnp.int32(max_rank // 8), rank_class.astype(jnp.int32))
    columns = lax.broadcasted_iota(jnp.int32, tile_scales.shape, 2)
    return jnp.where(columns < ranks[:, :, None], tile_scales, jnp.zeros_like(tile_scales))


def forward_all(direction_b, u_factors, v_factors, weights):
    pieces = lax.optimization_barrier(direction_b).astype(jnp.float32).reshape(FRAMES, TILE_COLS, TILE)

    def one_row(operands):
        left_row, right_row, weight_row = operands
        projected = jnp.einsum("fjm,jmr->fjr", pieces, right_row.astype(jnp.float32), precision=lax.Precision.HIGHEST)
        scaled = lax.optimization_barrier((projected * weight_row[None]).astype(jnp.bfloat16)).astype(jnp.float32)
        return jnp.einsum("fjr,jsr->fs", scaled, left_row.astype(jnp.float32), precision=lax.Precision.HIGHEST)

    blocks = lax.map(one_row, (u_factors, v_factors, weights))
    return jnp.transpose(blocks, (1, 0, 2)).reshape(FRAMES, SLOPES)


def backward_all(image_b, u_factors, v_factors, weights):
    pieces = lax.optimization_barrier(image_b).astype(jnp.float32).reshape(FRAMES, TILE_ROWS, TILE)
    pieces = jnp.transpose(pieces, (1, 0, 2))

    def add_row(totals, operands):
        left_row, right_row, weight_row, source_row = operands
        projected = jnp.einsum("fs,jsr->fjr", source_row, left_row.astype(jnp.float32), precision=lax.Precision.HIGHEST)
        scaled = lax.optimization_barrier((projected * weight_row[None]).astype(jnp.bfloat16)).astype(jnp.float32)
        return totals + jnp.einsum("fjr,jmr->fjm", scaled, right_row.astype(jnp.float32), precision=lax.Precision.HIGHEST), None

    start = jnp.zeros((FRAMES, TILE_COLS, TILE), jnp.float32)
    totals, unused = lax.scan(add_row, start, (u_factors, v_factors, weights, pieces))
    return totals.reshape(FRAMES, MODES)


def reference(u_factors, v_factors, tile_scales, rank_class, slopes):
    weights = rank_weights(tile_scales, rank_class)
    right_side = backward_all(slopes.astype(jnp.bfloat16), u_factors, v_factors, weights)
    solution_field = jnp.zeros_like(right_side)
    residual = right_side
    direction = right_side
    norm_now = jnp.sum(residual * residual, axis=1)
    for sweep in range(ITERS):
        forward_image = forward_all(direction.astype(jnp.bfloat16), u_factors, v_factors, weights)
        image_norm = jnp.sum(forward_image * forward_image, axis=1)
        dir_norm = jnp.sum(direction * direction, axis=1)
        operator_image = backward_all(forward_image.astype(jnp.bfloat16), u_factors, v_factors, weights) + damping * direction
        step_size = norm_now / (image_norm + damping * dir_norm + epsilon)
        solution_field = solution_field + step_size[:, None] * direction
        residual = residual - step_size[:, None] * operator_image
        norm_next = jnp.sum(residual * residual, axis=1)
        direction = residual + (norm_next / (norm_now + epsilon))[:, None] * direction
        norm_now = norm_next
    return solution_field, residual
```

```python
import functools

import jax
import jax.numpy as jnp
from jax import lax
from jax.experimental import pallas as pl
from jax.experimental.pallas import tpu as pltpu
from jax.sharding import PartitionSpec as P

GROUPS = 1

damping = 0.1
epsilon = 1e-06
MESH = pl.DeviceIdType.MESH
bf16 = jnp.bfloat16
f32 = jnp.float32


def lane_sums(value):
    total = value[:, 0:128]
    for start in range(128, value.shape[1], 128):
        total = total + value[:, start : start + 128]
    return total


def fold(value):
    return jnp.sum(value, axis=1, keepdims=True)


def kernel(sizes, u_hbm, v_hbm, scales, classes, slopes, x_ref, r_ref,
           u_vm, v_vm, wu, wv, hb, tb, pb, sib, hyp_s, hyp_r, full, own,
           sq, sq_r, hyq_s, hyq_r, csum, cs_s, cs_r, zb, zt, ch_s, ch_r, scal, own_scal,
           load_u, load_v, send_sem, recv_sem):
    R, C, G, TR, TC, T, K, F = sizes
    FG = F // G
    H = FG // 2
    phases = (R // 2).bit_length() - 1
    row = lax.axis_index("row")
    col = lax.axis_index("col")
    core = lax.rem(row, 2)
    chip = row // 2
    sibling = row + 1 - 2 * core

    def partner(bit):
        low = lax.rem(chip // (1 << bit), 2)
        return row + (1 - 2 * low) * (2 << bit)

    loads_u, loads_v = {}, {}
    for i in range(TR):
        for j in range(TC):
            loads_u[i, j] = pltpu.make_async_copy(
                u_hbm.at[i, j], u_vm.at[i, :, pl.ds(j * K, K)], load_u.at[i, j])
            loads_u[i, j].start()
    for j in range(TC):
        for i in range(TR):
            loads_v[i, j] = pltpu.make_async_copy(
                v_hbm.at[i, j], v_vm.at[j, :, pl.ds(i * K, K)], load_v.at[i, j])
            loads_v[i, j].start()

    barrier = pltpu.get_barrier_semaphore()
    pl.semaphore_signal(barrier, inc=1, device_id={"row": sibling}, device_id_type=MESH)
    for bit in range(phases):
        pl.semaphore_signal(barrier, inc=1, device_id={"row": partner(bit)}, device_id_type=MESH)

    @pl.when(col > 0)
    def _():
        pl.semaphore_signal(barrier, inc=1, device_id={"col": col - 1}, device_id_type=MESH)

    @pl.when(col < C - 1)
    def _():
        pl.semaphore_signal(barrier, inc=1, device_id={"col": col + 1}, device_id_type=MESH)

    lane = lax.broadcasted_iota(jnp.int32, (1, K), 1)
    least = ((lane >= K // 8).astype(jnp.int32) + (lane >= K // 4).astype(jnp.int32)
             + (lane >= K // 2).astype(jnp.int32))
    for i in range(TR):
        for j in range(TC):
            w = jnp.where(least <= classes[i, j], scales[i, j : j + 1, :], 0.0)
            wu[i : i + 1, j * K : (j + 1) * K] = w
            wv[j : j + 1, i * K : (i + 1) * K] = w

    @pl.when(col == 0)
    def _():
        for g in range(G):
            for a in range(2):
                ch_r[g, a, 0] = jnp.zeros_like(ch_r[g, a, 0])
                cs_r[g, a, 0] = jnp.zeros_like(cs_r[g, a, 0])

    @pl.when(col == C - 1)
    def _():
        for g in range(G):
            for a in range(2):
                ch_r[g, a, 1] = jnp.zeros_like(ch_r[g, a, 1])
                cs_r[g, a, 1] = jnp.zeros_like(cs_r[g, a, 1])

    count = [0]
    sent = []

    def ticket():
        count[0] += 1
        return count[0] - 1

    def remote(src, dst, number, device):
        return pltpu.make_async_remote_copy(
            src_ref=src, dst_ref=dst, send_sem=send_sem.at[number], recv_sem=recv_sem.at[number],
            device_id=device, device_id_type=MESH)

    mine = pl.ds(pl.multiple_of(core * H, H), H)
    theirs = pl.ds(pl.multiple_of((1 - core) * H, H), H)

    def push(src, dst, device):
        copy = remote(src, dst, ticket(), device)
        copy.start()
        sent.append((lambda: copy.wait_send(), None))
        return copy

    def chain(own_ref, s_ref, r_ref_, direction, number):
        up = (col > 0) if direction == 0 else (col < C - 1)
        down = (col < C - 1) if direction == 0 else (col > 0)
        to = lax.rem(col + 1, C) if direction == 0 else lax.rem(col + C - 1, C)

        def make():
            return remote(s_ref, r_ref_, number, {"col": to})

        @pl.when(up)
        def _():
            make().wait_recv()

        @pl.when(down)
        def _():
            s_ref[...] = (own_ref[...] + r_ref_[...].astype(f32)).astype(s_ref.dtype)
            make().start()

    def chain_all(own_ref, s_refs, r_refs, numbers, order):
        near = col < C // 2

        @pl.when(near)
        def _():
            chain(own_ref, s_refs[order], r_refs[order], order, numbers[order])

        @pl.when(jnp.logical_not(near))
        def _():
            chain(own_ref, s_refs[1 - order], r_refs[1 - order], 1 - order, numbers[1 - order])

    def note_chain(s_refs, r_refs, numbers):
        for d in range(2):
            def finish(d=d):
                remote(s_refs[d], r_refs[d], numbers[d], {"col": lax.rem(col + 1 + d * (C - 2), C)}).wait_send()
            sent.append((finish, (col < C - 1) if d == 0 else (col > 0)))

    first = [True] * (TR + TC)

    def h_stage(g, i, y):
        if first[i]:
            first[i] = False
            for j in range(TC):
                loads_u[i, j].wait()
        h = jnp.dot(y, u_vm[i], preferred_element_type=f32)
        h = (h * wu[i : i + 1, :]).astype(bf16)
        for j in range(TC):
            hb[g, j, :, i * K : (i + 1) * K] = h[:, j * K : (j + 1) * K]

    def t_stage(g, a, j):
        t = jnp.dot(full[g, a, :, j * T : (j + 1) * T], v_vm[j], preferred_element_type=f32)
        t = (t * wv[j : j + 1, :]).astype(bf16)
        for i in range(TR):
            tb[g, i, :, j * K : (j + 1) * K] = t[:, i * K : (i + 1) * K]

    def across(left, right):
        return lax.dot_general(left, right, (((1,), (1,)), ((), ())), preferred_element_type=f32)

    barrier_passed = [False]

    def process(g):
        frames = slice(g * FG, (g + 1) * FG)
        for i in range(TR):
            h_stage(g, i, slopes[frames, i * T : (i + 1) * T].astype(bf16))
        if not barrier_passed[0]:
            barrier_passed[0] = True
            pl.semaphore_wait(
                barrier, 1 + phases + (col > 0).astype(jnp.int32) + (col < C - 1).astype(jnp.int32))
        yield
        for a in range(3):
            yield from row_sum(g, a)
            if a < 2:
                yield from col_sum(g, a)

    def row_sum(g, a):
        copies = {}
        stages = phases + 3
        lags = [0, 2] + [2 + 3 * (n + 1) for n in range(phases)] + [4 + 3 * phases]

        def bit_of(j, n):
            return n if j % 2 == 0 else phases - 1 - n

        def cols(j):
            return pl.ds(j * T, T)

        def scalar_stage(k):
            q = a - 1
            if k == 0:
                copies["s", 0] = push(sq.at[g, q, theirs], sq_r.at[g, q], {"row": sibling})
            elif k <= phases + 1:
                copies["s", k - 1].wait_recv()
                if k == 1:
                    total = sq[g, q, mine] + sq_r[g, q]
                else:
                    total = hyq_s[g, q, k - 2] + hyq_r[g, q, k - 2]
                if k <= phases:
                    hyq_s[g, q, k - 1] = total
                    copies["s", k] = push(hyq_s.at[g, q, k - 1], hyq_r.at[g, q, k - 1], {"row": partner(k - 1)})
                else:
                    image_norm = fold(total)
                    now = scal[g, 0, mine] if a == 1 else scal[g, 1, mine]
                    now = now[:, 0:1]
                    if a == 1:
                        dir_norm = now
                    else:
                        rr0 = scal[g, 0, mine][:, 0:1]
                        beta = now / (rr0 + epsilon)
                        dir_norm = now + 2 * beta * scal[g, 2, mine][:, 0:1] + beta * beta * rr0
                        own_scal[g, 2] = jnp.broadcast_to(beta, (H, 128))
                    alpha = now / (image_norm + damping * dir_norm + epsilon)
                    own_scal[g, q] = jnp.broadcast_to(alpha, (H, 128))

        def finish(j, q):
            at = slice(j * T, (j + 1) * T)
            if a == 0:
                own[g, 0, :, at] = q
                full[g, 0, mine, at] = q.astype(bf16)
            elif a == 1:
                b = own[g, 0, :, at]
                res = b - own_scal[g, 0][:, 0:1] * (q + damping * b)
                own[g, 1, :, at] = res
                full[g, 1, mine, at] = res.astype(bf16)
            else:
                b = own[g, 0, :, at]
                res = own[g, 1, :, at]
                alpha0, alpha1, beta = (own_scal[g, n][:, 0:1] for n in range(3))
                direction = res + beta * b
                rows = pl.ds(pl.multiple_of(g * FG + core * H, H), H)
                x_ref[rows, at] = alpha0 * b + alpha1 * direction
                r_ref[rows, at] = res - alpha1 * (q + damping * direction)
                copies[j, "x"] = push(x_ref.at[rows, cols(j)], x_ref.at[rows, cols(j)], {"row": sibling})
                copies[j, "r"] = push(r_ref.at[rows, cols(j)], r_ref.at[rows, cols(j)], {"row": sibling})
                return
            copies[j, "g"] = push(full.at[g, a, mine, cols(j)], full.at[g, a, mine, cols(j)], {"row": sibling})

        def stage(j, k):
            at = slice(j * T, (j + 1) * T)
            if k == 0:
                if first[TR + j]:
                    first[TR + j] = False
                    for i in range(TR):
                        loads_v[i, j].wait()
                pb[g, a, :, at] = across(hb[g, j], v_vm[j])
                copies[j, 0] = push(pb.at[g, a, theirs, cols(j)], sib.at[g, a, :, cols(j)], {"row": sibling})
            elif k <= phases + 1:
                copies[j, k - 1].wait_recv()
                if k == 1:
                    total = pb[g, a, mine, at] + sib[g, a, :, at]
                else:
                    total = hyp_s[g, a, k - 2, :, at].astype(f32) + hyp_r[g, a, k - 2, :, at].astype(f32)
                if k <= phases:
                    hyp_s[g, a, k - 1, :, at] = total.astype(bf16)
                    copies[j, k] = push(hyp_s.at[g, a, k - 1, :, cols(j)], hyp_r.at[g, a, k - 1, :, cols(j)],
                                        {"row": partner(bit_of(j, k - 1))})
                else:
                    finish(j, total)
            elif a == 2:
                copies[j, "x"].wait_recv()
                copies[j, "r"].wait_recv()
            else:
                copies[j, "g"].wait_recv()
                t_stage(g, a, j)
                now = full[g, a, :, at].astype(f32)
                terms = [lane_sums(now * now)]
                if a == 1:
                    terms.append(lane_sums(now * full[g, 0, :, at].astype(f32)))
                for n, term in enumerate(terms):
                    csum[g, a, n] = term if j == 0 else csum[g, a, n] + term

        for slot in range(TC + lags[-1]):
            for k in range(stages - 1, 0, -1):
                if a > 0 and slot == lags[k] and k <= phases + 1:
                    scalar_stage(k)
                if 0 <= slot - lags[k] < TC:
                    stage(slot - lags[k], k)
            if a > 0 and slot == 0:
                scalar_stage(0)
            if slot < TC:
                stage(slot, 0)
            yield

    def col_sum(g, a):
        numbers = [(ticket(), ticket()) for _ in range(TR + 1)]
        n_sums = 1 + a
        part = pl.ds(0, n_sums)

        def refs(i):
            if i < 0:
                return (csum.at[g, a, part], [cs_s.at[g, a, d, part] for d in range(2)],
                        [cs_r.at[g, a, d, part] for d in range(2)])
            at = pl.ds(i * T, T)
            return (zb.at[g, a, :, at], [ch_s.at[g, a, d, :, at] for d in range(2)],
                    [ch_r.at[g, a, d, :, at] for d in range(2)])

        edge = jnp.logical_or(col == 0, col == C - 1)

        def stage(i, k):
            own_ref, s_refs, r_refs = refs(i)
            if k == 0:
                if i >= 0:
                    zb[g, a, :, i * T : (i + 1) * T] = across(tb[g, i], u_vm[i])
                note_chain(s_refs, r_refs, numbers[i])

                @pl.when(edge)
                def _():
                    chain_all(own_ref, s_refs, r_refs, numbers[i], 0)
            elif k == 1:
                @pl.when(jnp.logical_not(edge))
                def _():
                    chain_all(own_ref, s_refs, r_refs, numbers[i], 0)
            elif k == 2:
                chain_all(own_ref, s_refs, r_refs, numbers[i], 1)
            elif i < 0:
                for n in range(n_sums):
                    total = csum[g, a, n] + cs_r[g, a, 0, n] + cs_r[g, a, 1, n]
                    scal[g, a + n] = jnp.broadcast_to(fold(total), (FG, 128))
            else:
                at = slice(i * T, (i + 1) * T)
                z = zb[g, a, :, at] + ch_r[g, a, 0, :, at].astype(f32) + ch_r[g, a, 1, :, at].astype(f32)
                if a == 0:
                    zt[g, :, at] = z
                else:
                    beta = scal[g, 1][:, 0:1] / (scal[g, 0][:, 0:1] + epsilon)
                    z = z + beta * zt[g, :, at]
                term = lane_sums(z * z)
                sq[g, a] = term if i == 0 else sq[g, a] + term
                h_stage(g, i, z.astype(bf16))

        lags = [0, 1, 2, 3]
        for slot in range(TR + lags[-1] + 1):
            for k in range(3, -1, -1):
                if slot == max(lags[k], 0):
                    stage(-1, k)
                if 0 <= slot - lags[k] < TR:
                    stage(slot - lags[k], k)
            yield

    running = [process(g) for g in range(G)]
    ahead = 20
    for _ in range(ahead if G > 1 else 0):
        next(running[0])
    while running:
        for one in list(running):
            try:
                next(one)
            except StopIteration:
                running.remove(one)

    for finish, condition in sent:
        if condition is None:
            finish()
        else:
            pl.when(condition)(finish)


def per_device(u_factors, v_factors, tile_scales, rank_class, slopes):
    R, C, G = lax.axis_size("row"), lax.axis_size("col"), GROUPS
    TR, TC, T, K = u_factors.shape
    F = slopes.shape[0]
    FG, H = F // G, F // G // 2
    NM, NS = TC * T, TR * T
    phases = (R // 2).bit_length() - 1
    copies = G * (3 * (TC * (2 + phases)) + TC + 2 * (1 + phases) + 2 * 2 * (TR + 1))
    vm = pltpu.VMEM
    scratch = [
        vm((TR, T, TC * K), bf16), vm((TC, T, TR * K), bf16),
        vm((TR, TC * K), f32), vm((TC, TR * K), f32),
        vm((G, TC, FG, TR * K), bf16), vm((G, TR, FG, TC * K), bf16),
        vm((G, 3, FG, NM), f32), vm((G, 3, H, NM), f32),
        vm((G, 3, phases, H, NM), bf16), vm((G, 3, phases, H, NM), bf16),
        vm((G, 2, FG, NM), bf16), vm((G, 2, H, NM), f32),
        vm((G, 2, FG, 128), f32), vm((G, 2, H, 128), f32),
        vm((G, 2, phases, H, 128), f32), vm((G, 2, phases, H, 128), f32),
        vm((G, 2, 2, FG, 128), f32), vm((G, 2, 2, 2, FG, 128), f32), vm((G, 2, 2, 2, FG, 128), f32),
        vm((G, 2, FG, NS), f32), vm((G, FG, NS), f32),
        vm((G, 2, 2, FG, NS), bf16), vm((G, 2, 2, FG, NS), bf16),
        vm((G, 3, FG, 128), f32), vm((G, 3, H, 128), f32),
        pltpu.SemaphoreType.DMA((TR, TC)), pltpu.SemaphoreType.DMA((TR, TC)),
        pltpu.SemaphoreType.DMA((copies,)), pltpu.SemaphoreType.DMA((copies,)),
    ]
    out = jax.ShapeDtypeStruct((F, NM), f32)
    return pl.pallas_call(
        functools.partial(kernel, (R, C, G, TR, TC, T, K, F)),
        out_shape=(out, out),
        in_specs=[
            pl.BlockSpec(memory_space=pl.ANY), pl.BlockSpec(memory_space=pl.ANY),
            pl.BlockSpec(memory_space=pltpu.VMEM), pl.BlockSpec(memory_space=pltpu.SMEM),
            pl.BlockSpec(memory_space=pltpu.VMEM),
        ],
        out_specs=[pl.BlockSpec(memory_space=pltpu.VMEM)] * 2,
        scratch_shapes=scratch,
        compiler_params=pltpu.CompilerParams(
            collective_id=0, has_side_effects=True, vmem_limit_bytes=56 * 2**20),
    )(u_factors, v_factors, tile_scales, rank_class, slopes)


def solution(mesh):
    return jax.shard_map(
        per_device,
        mesh=mesh,
        in_specs=(
            P("row", "col", None, None),
            P("row", "col", None, None),
            P("row", "col", None),
            P("row", "col"),
            P(None, "row"),
        ),
        out_specs=(P(None, "col"), P(None, "col")),
        check_vma=False,
    )
```
